32 devices in a mesh: row: 8 (over z, x), col: 4 (over y, core).
Axes of the slice: x: 2, y: 2, z: 4, core: 2. Of those that a mesh axis runs over, the one named last changes fastest.
Arguments:
- start_block: float32 [16, 73728], P(None, ('row', 'col'))
- start_search: float32 [16, 73728], P(None, ('row', 'col')), may hold values from -6 to 6
- precond: float32 [73728], P(('row', 'col')), may hold values from 0.25 to 1
- diag_energy: float32 [73728], P(('row', 'col')), may hold values from 1 to 16
- blocks: bfloat16 [8, 4, 64, 128, 128], P('row', 'col'), may hold values from -0.375 to 0.375
- row_index: int32 [8, 4, 64], P('row', 'col'), may hold values from 0 to 71
- col_index: int32 [8, 4, 64], P('row', 'col'), may hold values from 0 to 143
- live_count: int32 [8, 4], P('row', 'col'), may hold values from 16 to 64, as said below
- ritz_coeffs: float32 [2, 3, 16, 16], replicated
Outputs:
- final_block: float32 [16, 73728], P(None, ('row', 'col'))
- ritz_values: float32 [16], replicated
The draws below stay inside these ranges and needn't reach their ends.
Inputs may be any that keep to these rules, and one draw needn't show every extreme that they name: Every live_count is at least 16, and some device has all 64 slots live.
All inputs are finite; a program needn't handle non-finite values.
Results may differ from the reference program's by a relative error of at most 0.019.
Values may be sent and summed in bfloat16 or wider, within the bound.
A program may use at most 64 MiB of HBM per device.

```python
import math
import jax
import jax.numpy as jnp
from jax import lax

K = 16
BS = 128
CB = 18
NNZB = 64
ITERS = 2
ROWS_DEV = 2304
NDIM = 73728
N_ROW = 8
N_COL = 4


def draw_start_block(key, part):
    key = jax.random.fold_in(key, 1)
    profile = 1.0 + 2.0 * jnp.arange(NDIM, dtype=jnp.float32) / NDIM
    values = jax.random.normal(key, (K, NDIM), jnp.float32)
    return values * profile[None, :]


def draw_live_count(key, part):
    key = jax.random.fold_in(key, 3)
    first, second = jax.random.split(key)
    counts = jax.random.randint(first, (N_ROW * N_COL,), NNZB // 4, NNZB + 1)
    chosen = jax.random.randint(second, (), 0, N_ROW * N_COL)
    counts = jnp.where(jnp.arange(N_ROW * N_COL) == chosen, NNZB, counts)
    return counts.reshape(N_ROW, N_COL).astype(jnp.int32)


def draw_ritz_coeffs(key, part):
    key = jax.random.fold_in(key, 2)
    gaussian = jax.random.normal(key, (ITERS, 3, K, K), jnp.float32)
    identity = jnp.eye(K, dtype=jnp.float32)
    scales = jnp.array([1.0, 0.6, 0.6], jnp.float32)[None, :, None, None]
    return scales * (identity[None, None] + 0.3 * gaussian)


def with_ends(result, own_key, low, high):
    longest = result.shape.index(max(result.shape))
    spots = []
    for shift in (0, 1):
        where = [jax.random.randint(jax.random.fold_in(own_key, axis), (), 0, length) for axis, length in enumerate(result.shape)]
        where[longest] = (where[longest] + shift) % result.shape[longest]
        spots.append(tuple(where))
    return result.at[spots[0]].set(low).at[spots[1]].set(high)


def shard_levels(own_key, shape, pieces, least, high):
    loudness = 1.0
    for dim, blocks in pieces:
        steps = jax.random.uniform(jax.random.fold_in(jax.random.fold_in(own_key, 6), dim), (blocks,), jnp.float32, least / len(pieces), high / len(pieces))
        loudness = loudness * jnp.repeat(jnp.exp(steps), shape[dim] // blocks).reshape((-1,) + (1,) * (len(shape) - 1 - dim))
    return loudness


def centred(key, shape, width, most, cuts=(), kind=jnp.bfloat16):
    entries = jax.random.normal(key, shape, jnp.float32) * width
    if len(cuts) > 0:
        entries = shard_levels(key, shape, cuts, -0.22, 0.18) * entries
    return jnp.clip(entries, min=-most, max=most).astype(kind)


def setup_inputs(seed: int = 0) -> dict:
    key_list = jax.random.split(jax.random.key(seed), 10)
    start_block = draw_start_block(jax.random.fold_in(key_list[9], 71), 0)
    start_search = centred(key_list[1], (K, NDIM), 1.0, 6.0, ((1, 32),), jnp.float32)
    precond = jnp.clip(jnp.exp(math.log(1.0) - 1.3862944 * jax.random.uniform(key_list[2], (NDIM,), jnp.float32) ** shard_levels(key_list[2], (NDIM,), ((0, 32),), -0.2, 0.2)), 0.25, 1.0)
    diag_energy = jnp.clip(jnp.exp(math.log(16.0) - 2.7725887 * jax.random.uniform(key_list[3], (NDIM,), jnp.float32) ** shard_levels(key_list[3], (NDIM,), ((0, 32),), -0.2, 0.2)), 1.0, 16.0)
    blocks = centred(key_list[4], (N_ROW, N_COL, NNZB, BS, BS), (2 * BS * NNZB // (N_COL * CB)) ** -0.5, 0.375, ((0, 8), (1, 4)))
    row_index = with_ends(jax.random.randint(key_list[5], (N_ROW, N_COL, NNZB), 0, N_COL * CB), jax.random.fold_in(key_list[5], 1), 0, (N_COL * CB) - 1).astype(jnp.int32)
    col_index = with_ends(jax.random.randint(key_list[6], (N_ROW, N_COL, NNZB), 0, N_ROW * CB), jax.random.fold_in(key_list[6], 1), 0, (N_ROW * CB) - 1).astype(jnp.int32)
    live_count = draw_live_count(jax.random.fold_in(key_list[9], 71), 0)
    ritz_coeffs = draw_ritz_coeffs(jax.random.fold_in(key_list[9], 71), 0)
    return {"start_block": start_block, "start_search": start_search, "precond": precond, "diag_energy": diag_energy, "blocks": blocks, "row_index": row_index, "col_index": col_index, "live_count": live_count, "ritz_coeffs": ritz_coeffs}


def local_terms(tile_set, row_ids, col_ids, live, col_tiles, row_tiles):
    slots = tile_set.shape[0]
    alive = jnp.arange(slots) < live
    tile_f = tile_set.astype(jnp.float32)
    gathered_col = jnp.take(col_tiles, col_ids, axis=0).astype(jnp.float32)
    gathered_row = jnp.take(row_tiles, row_ids, axis=0).astype(jnp.float32)
    direct = jnp.einsum('bij,bkj->bki', tile_f, gathered_col)
    transposed = jnp.einsum('bij,bki->bkj', tile_f, gathered_row)
    nrows = row_tiles.shape[0]
    ncols = col_tiles.shape[0]
    hot_rows = ((jnp.arange(nrows)[:, None] == row_ids[None, :]) & alive[None, :]).astype(jnp.float32)
    hot_cols = ((jnp.arange(ncols)[:, None] == col_ids[None, :]) & alive[None, :]).astype(jnp.float32)
    row_total = jnp.dot(hot_rows, direct.reshape(slots, -1), precision=lax.Precision.HIGHEST)
    col_total = jnp.dot(hot_cols, transposed.reshape(slots, -1), precision=lax.Precision.HIGHEST)
    return row_total, col_total


def apply_operator(vec_bf, diag_energy, blocks, row_index, col_index, live_count):
    vec_count = vec_bf.shape[0]
    grid_vec = vec_bf.reshape(vec_count, N_ROW, N_COL, ROWS_DEV)
    flat_blocks = blocks.reshape(N_ROW * N_COL, NNZB, BS, BS)
    flat_rows = row_index.reshape(N_ROW * N_COL, NNZB)
    flat_cols = col_index.reshape(N_ROW * N_COL, NNZB)
    flat_live = live_count.reshape(N_ROW * N_COL)

    def device_terms(device_flat, totals):
        row_id = device_flat // N_COL
        col_id = device_flat % N_COL
        col_tiles = jnp.take(grid_vec, col_id, axis=2).reshape(vec_count, N_ROW * CB, BS).transpose(1, 0, 2)
        row_tiles = jnp.take(grid_vec, row_id, axis=1).reshape(vec_count, N_COL * CB, BS).transpose(1, 0, 2)
        row_total, col_total = local_terms(flat_blocks[device_flat], flat_rows[device_flat], flat_cols[device_flat], flat_live[device_flat], col_tiles, row_tiles)
        direct_sum = row_total.reshape(N_COL * CB, vec_count, BS).transpose(1, 0, 2).reshape(vec_count, N_COL, ROWS_DEV)
        trans_sum = col_total.reshape(N_ROW * CB, vec_count, BS).transpose(1, 0, 2).reshape(vec_count, N_ROW, ROWS_DEV)
        totals = totals.at[:, row_id].add(direct_sum)
        totals = totals.at[:, :, col_id].add(trans_sum)
        return totals

    totals = lax.fori_loop(0, N_ROW * N_COL, device_terms, jnp.zeros((vec_count, N_ROW, N_COL, ROWS_DEV), jnp.float32))
    return totals.reshape(vec_count, NDIM) + diag_energy[None, :] * vec_bf.astype(jnp.float32)


def quotients(block, image):
    return jnp.sum(block * image, axis=1) / jnp.sum(block * block, axis=1)


def combine_three(coef_a, first, coef_b, second, coef_c, third):
    hi = lax.Precision.HIGHEST
    return jnp.dot(coef_a.T, first, precision=hi) + jnp.dot(coef_b.T, second, precision=hi) + jnp.dot(coef_c.T, third, precision=hi)


def reference(start_block, start_search, precond, diag_energy, blocks, row_index, col_index, live_count, ritz_coeffs):
    hi = lax.Precision.HIGHEST
    block = start_block
    search = start_search
    image_x = apply_operator(block.astype(jnp.bfloat16), diag_energy, blocks, row_index, col_index, live_count)
    image_p = apply_operator(search.astype(jnp.bfloat16), diag_energy, blocks, row_index, col_index, live_count)
    for iteration in range(ITERS):
        ritz_now = quotients(block, image_x)
        residual = (image_x - ritz_now[:, None] * block) * precond[None, :]
        image_r = apply_operator(residual.astype(jnp.bfloat16), diag_energy, blocks, row_index, col_index, live_count)
        coef_x = ritz_coeffs[iteration, 0]
        coef_w = ritz_coeffs[iteration, 1]
        coef_p = ritz_coeffs[iteration, 2]
        new_block = combine_three(coef_x, block, coef_w, residual, coef_p, search)
        new_search = jnp.dot(coef_w.T, residual, precision=hi) + jnp.dot(coef_p.T, search, precision=hi)
        new_image_x = combine_three(coef_x, image_x, coef_w, image_r, coef_p, image_p)
        new_image_p = jnp.dot(coef_w.T, image_r, precision=hi) + jnp.dot(coef_p.T, image_p, precision=hi)
        block, search, image_x, image_p = new_block, new_search, new_image_x, new_image_p
    return block, quotients(block, image_x)
```

```python
import functools

import jax
import jax.numpy as jnp
from jax import lax
from jax.experimental import pallas as pl
from jax.experimental.pallas import tpu as pltpu
from jax.sharding import PartitionSpec as P

ITERS = 2
BS = 128
GROUP = 9
F32 = jnp.float32
BF16 = jnp.bfloat16
HI = lax.Precision.HIGHEST
MESH = pl.DeviceIdType.MESH


def dot_t(left, right, precision=None):
    return lax.dot_general(
        left, right, (((1,), (1,)), ((), ())), precision=precision, preferred_element_type=F32
    )


def dot_n(left, right, precision=None):
    return lax.dot_general(
        left, right, (((1,), (0,)), ((), ())), precision=precision, preferred_element_type=F32
    )


def kernel(
    n_row, n_col, nb, k, slots,
    block_in, search_in, precond_in, diag_in, blocks, row_smem, col_smem, live_smem,
    row_ids, col_ids, coeffs,
    block_out, ritz_out,
    sent, row_g, col_g, row_b, col_b, terms, row_acc, col_acc, row_send, col_send,
    row_part, col_part, scal, row_scal, col_scal,
    row_ssem, row_rsem, col_ssem, col_rsem,
):
    r = lax.axis_index("row")
    c = lax.axis_index("col")
    rows = nb * k
    grows = GROUP * k

    barrier = pltpu.get_barrier_semaphore()
    for d in range(1, n_row):
        pl.semaphore_signal(barrier, inc=1, device_id=(lax.rem(r + d, n_row), c), device_id_type=MESH)
    for d in range(1, n_col):
        pl.semaphore_signal(barrier, inc=1, device_id=(r, lax.rem(c + d, n_col)), device_id_type=MESH)

    def row_copy(phase, d, src, dst):
        return pltpu.make_async_remote_copy(
            src_ref=src, dst_ref=dst, send_sem=row_ssem.at[phase, d], recv_sem=row_rsem.at[phase, d],
            device_id=(lax.rem(r + d, n_row), c), device_id_type=MESH,
        )

    def col_copy(phase, d, src, dst):
        return pltpu.make_async_remote_copy(
            src_ref=src, dst_ref=dst, send_sem=col_ssem.at[phase, d], recv_sem=col_rsem.at[phase, d],
            device_id=(r, lax.rem(c + d, n_col)), device_id_type=MESH,
        )

    def start_gather(phase, values):
        sent[phase] = values
        by_col = [
            col_copy(phase, d, sent.at[phase], row_g.at[phase, pl.ds(c * nb, nb)]) for d in range(1, n_col)
        ]
        by_row = [
            row_copy(phase, d, sent.at[phase], col_g.at[phase, pl.ds(r * nb, nb)]) for d in range(1, n_row)
        ]
        for copy in by_col + by_row:
            copy.start()
        row_g[phase, pl.ds(c * nb, nb)] = values
        col_g[phase, pl.ds(r * nb, nb)] = values
        return by_col, by_row

    def wait_all(copies):
        for copy in copies:
            copy.wait()

    live = live_smem[0, 0]

    def hot(ids, count):
        alive = lax.broadcasted_iota(jnp.int32, (count, slots), 1) < live
        same = lax.broadcasted_iota(jnp.int32, (count, slots), 0) == ids
        one = jnp.where(same & alive, 1.0, 0.0).astype(BF16)
        return jnp.concatenate([one, one], axis=1)

    def slot_products(phase, source, index, dot):
        def body(group, carry):
            for u in range(8):
                s = group * 8 + u
                terms[pl.ds(pl.multiple_of(s * k, k), k), :] = dot(source[phase, index[0, s]], blocks[s])
            return carry

        lax.fori_loop(0, slots // 8, body, 0)

    def slot_sums(hots, acc, count):
        for q in range(k):
            part = terms[pl.ds(q, slots, stride=k), :]
            high = part.astype(BF16)
            low = (part - high.astype(F32)).astype(BF16)
            acc[pl.ds(q, count, stride=k), :] = dot_n(hots, jnp.concatenate([high, low], axis=0))

    def send_parts(phase, acc, out, part, count, me, make):
        out[phase] = acc[...].astype(BF16).reshape(count * nb, k, BS)
        copies = [
            make(3 + phase, d, out.at[phase, pl.ds(lax.rem(me + d, count) * nb, nb)], part.at[phase, me])
            for d in range(1, count)
        ]
        for copy in copies:
            copy.start()
        part[phase, me] = out[phase, pl.ds(me * nb, nb)]
        return copies

    def part_sum(phase, part, count):
        total = part[phase, 0].astype(F32)
        for i in range(1, count):
            total = total + part[phase, i].astype(F32)
        return total

    def inner(gathered, acc, count):
        total = jnp.zeros((k, BS), F32)
        for i in range(0, count * nb, GROUP):
            total = total + jnp.sum(
                gathered(i).astype(F32) * acc[i * k : (i + GROUP) * k, :].reshape(GROUP, k, BS), axis=0
            )
        return total

    def local_dot(left, right):
        return jnp.sum(left * right, axis=0)

    lane = lax.broadcasted_iota(jnp.int32, (k, BS), 1)

    def reduce_row(phase, num, den):
        packed = jnp.where(
            lane < BS // 2, jnp.sum(num, axis=1, keepdims=True), jnp.sum(den, axis=1, keepdims=True)
        )
        scal[0, phase] = packed
        row_scal[phase, r] = packed
        copies = [row_copy(5 + phase, d, scal.at[0, phase], row_scal.at[phase, r]) for d in range(1, n_row)]
        for copy in copies:
            copy.start()
        return copies

    def reduce_col(phase, copies):
        wait_all(copies)
        packed = jnp.sum(row_scal[phase], axis=0)
        scal[1, phase] = packed
        col_scal[phase, c] = packed
        copies = [col_copy(5 + phase, d, scal.at[1, phase], col_scal.at[phase, c]) for d in range(1, n_col)]
        for copy in copies:
            copy.start()
        wait_all(copies)
        total = jnp.sum(col_scal[phase], axis=0)
        return total[:, 0:1] / total[:, BS // 2 : BS // 2 + 1]

    def tiles(flat):
        return jnp.stack([flat[:, j * BS : (j + 1) * BS] for j in range(nb)], axis=0)

    start = block_in[...]
    block = tiles(start)
    pl.semaphore_wait(barrier, n_row + n_col - 2)
    by_col, by_row = start_gather(0, block.astype(BF16))

    search = tiles(search_in[...])
    precond = precond_in[...].reshape(nb, 1, BS)
    diag = diag_in[...].reshape(nb, 1, BS)
    hot_rows = hot(row_ids[...], n_col * nb)
    hot_cols = hot(col_ids[...], n_row * nb)

    spread = (
        lax.broadcasted_iota(jnp.int32, (grows, k), 0) % k == lax.broadcasted_iota(jnp.int32, (grows, k), 1)
    ).astype(F32)
    same_group = (
        lax.broadcasted_iota(jnp.int32, (grows, grows), 0) // k
        == lax.broadcasted_iota(jnp.int32, (grows, grows), 1) // k
    )

    def expand(coef):
        wide = dot_t(dot_t(spread, coef, HI), spread, HI)
        return jnp.where(same_group, wide, 0.0)

    mats = [[expand(coeffs[i, j]) for j in range(3)] for i in range(ITERS)]

    def combine(mat, values):
        flat = values.reshape(rows, BS)
        return jnp.concatenate(
            [dot_n(mat, flat[i : i + grows], HI) for i in range(0, rows, grows)], axis=0
        ).reshape(nb, k, BS)

    def combine_gathered(mat, values):
        high = mat.astype(BF16)
        low = (mat - high.astype(F32)).astype(BF16)
        flat = values.reshape(grows, BS)
        return (dot_n(high, flat) + dot_n(low, flat)).reshape(GROUP, k, BS)

    def operator(phase, by_col, by_row, send):
        wait_all(by_col)
        slot_products(phase, row_g, row_smem, dot_n)
        slot_sums(hot_cols, col_acc, n_row * nb)
        row_parts = send_parts(phase, col_acc, col_send, col_part, n_row, r, row_copy) if send else []
        wait_all(by_row)
        slot_products(phase, col_g, col_smem, dot_t)
        slot_sums(hot_rows, row_acc, n_col * nb)
        col_parts = send_parts(phase, row_acc, row_send, row_part, n_col, c, col_copy) if send else []
        return row_parts + col_parts

    parts = operator(0, by_col, by_row, True)
    own = diag * sent[0].astype(F32)
    num = (
        local_dot(block, own)
        + inner(lambda i: row_g[0, i : i + GROUP], row_acc, n_col)
        + inner(lambda i: col_g[0, i : i + GROUP], col_acc, n_row)
    )
    copies = reduce_row(0, num, local_dot(block, block))
    ritz = reduce_col(0, copies)
    wait_all(parts)
    image = own + part_sum(0, row_part, n_col) + part_sum(0, col_part, n_row)

    for i in range(ITERS):
        mat_x, mat_w, mat_p = mats[i]
        phase = i + 1
        residual = (image - ritz[None] * block) * precond
        search = combine(mat_w, residual) + combine(mat_p, search)
        by_col, by_row = start_gather(phase, search.astype(BF16))
        block = combine(mat_x, block) + search
        own = diag * sent[phase].astype(F32)
        image = combine(mat_x, image) + own
        num = local_dot(block, image)
        den = local_dot(block, block)
        for gathered, total, count in ((row_g, row_b, n_col), (col_g, col_b, n_row)):
            for g in range(0, count * nb, GROUP):
                old = gathered[0, g : g + GROUP] if i == 0 else total[g : g + GROUP]
                total[g : g + GROUP] = combine_gathered(mat_x, old).astype(BF16)
        if i == ITERS - 1:
            for j in range(nb):
                block_out[:, j * BS : (j + 1) * BS] = block[j]
        parts = operator(phase, by_col, by_row, i < ITERS - 1)
        for gathered, total, count in ((row_g, row_b, n_col), (col_g, col_b, n_row)):
            for g in range(0, count * nb, GROUP):
                total[g : g + GROUP] = (
                    total[g : g + GROUP].astype(F32) + gathered[phase, g : g + GROUP].astype(F32)
                ).astype(BF16)
        num = (
            num
            + inner(lambda g: row_b[g : g + GROUP], row_acc, n_col)
            + inner(lambda g: col_b[g : g + GROUP], col_acc, n_row)
        )
        copies = reduce_row(phase, num, den)
        ritz = reduce_col(phase, copies)
        if i < ITERS - 1:
            wait_all(parts)
            image = image + part_sum(phase, row_part, n_col) + part_sum(phase, col_part, n_row)

    ritz_out[...] = jnp.broadcast_to(ritz, (k, BS))


def on_device(
    n_row, n_col, start_block, start_search, precond, diag_energy, blocks, row_index, col_index,
    live_count, ritz_coeffs,
):
    k, length = start_block.shape
    nb = length // BS
    slots = blocks.shape[2]
    phases = ITERS + 1
    vmem = pl.BlockSpec(memory_space=pltpu.VMEM)
    smem = pl.BlockSpec(memory_space=pltpu.SMEM)
    row_ids = row_index[0]
    col_ids = col_index[0]
    block, ritz = pl.pallas_call(
        functools.partial(kernel, n_row, n_col, nb, k, slots),
        out_shape=(
            jax.ShapeDtypeStruct((k, length), F32),
            jax.ShapeDtypeStruct((k, BS), F32),
        ),
        in_specs=[vmem] * 5 + [smem] * 3 + [vmem] * 3,
        out_specs=(vmem, vmem),
        scratch_shapes=[
            pltpu.VMEM((phases, nb, k, BS), BF16),
            pltpu.VMEM((phases, n_col * nb, k, BS), BF16),
            pltpu.VMEM((phases, n_row * nb, k, BS), BF16),
            pltpu.VMEM((n_col * nb, k, BS), BF16),
            pltpu.VMEM((n_row * nb, k, BS), BF16),
            pltpu.VMEM((slots * k, BS), F32),
            pltpu.VMEM((n_col * nb * k, BS), F32),
            pltpu.VMEM((n_row * nb * k, BS), F32),
            pltpu.VMEM((phases - 1, n_col * nb, k, BS), BF16),
            pltpu.VMEM((phases - 1, n_row * nb, k, BS), BF16),
            pltpu.VMEM((phases - 1, n_col, nb, k, BS), BF16),
            pltpu.VMEM((phases - 1, n_row, nb, k, BS), BF16),
            pltpu.VMEM((2, phases, k, BS), F32),
            pltpu.VMEM((phases, n_row, k, BS), F32),
            pltpu.VMEM((phases, n_col, k, BS), F32),
            pltpu.SemaphoreType.DMA((8, n_row)),
            pltpu.SemaphoreType.DMA((8, n_row)),
            pltpu.SemaphoreType.DMA((8, n_col)),
            pltpu.SemaphoreType.DMA((8, n_col)),
        ],
        compiler_params=pltpu.CompilerParams(
            collective_id=0, has_side_effects=True, vmem_limit_bytes=48 * 1024 * 1024
        ),
    )(
        start_block, start_search, precond.reshape(nb, BS), diag_energy.reshape(nb, BS), blocks[0, 0],
        row_ids, col_ids, live_count, row_ids, col_ids, ritz_coeffs,
    )
    return block, ritz[:, 0]


def solution(mesh):
    placed = (
        P(None, ("row", "col")),
        P(None, ("row", "col")),
        P(("row", "col")),
        P(("row", "col")),
        P("row", "col", None, None, None),
        P("row", "col", None),
        P("row", "col", None),
        P("row", "col"),
        P(),
    )
    return jax.shard_map(
        functools.partial(on_device, mesh.shape["row"], mesh.shape["col"]),
        mesh=mesh,
        in_specs=placed,
        out_specs=(P(None, ("row", "col")), P()),
        check_vma=False,
    )
```

```python
import functools

import jax
import jax.numpy as jnp
from jax import lax
from jax.experimental import pallas as pl
from jax.experimental.pallas import tpu as pltpu
from jax.sharding import PartitionSpec as P

ITERS = 2
BS = 128
GROUP = 9
F32 = jnp.float32
BF16 = jnp.bfloat16
HI = lax.Precision.HIGHEST
MESH = pl.DeviceIdType.MESH


def dot_t(left, right, precision=None):
    return lax.dot_general(
        left, right, (((1,), (1,)), ((), ())), precision=precision, preferred_element_type=F32
    )


def dot_n(left, right, precision=None):
    return lax.dot_general(
        left, right, (((1,), (0,)), ((), ())), precision=precision, preferred_element_type=F32
    )


def kernel(
    n_row, n_col, nb, k, slots,
    block_hbm, search_hbm, precond_hbm, diag_hbm, blocks_hbm, row_ids_hbm, col_ids_hbm, coeffs_hbm,
    row_smem, col_smem, live_smem,
    block_out, ritz_out,
    sent, row_g, col_g, row_b, col_b, terms, row_acc, col_acc, row_send, col_send,
    row_part, col_part, scal, row_scal, col_scal,
    x_part, z_send, row_ssem, row_rsem, col_ssem, col_rsem,
    block_in, search_in, precond_in, diag_in, blocks, row_ids, col_ids, coeffs, load_sem,
):
    loads = [
        pltpu.make_async_copy(src, dst, load_sem.at[i])
        for i, (src, dst) in enumerate((
            (block_hbm, block_in), (search_hbm, search_in), (precond_hbm, precond_in),
            (diag_hbm, diag_in), (blocks_hbm, blocks), (row_ids_hbm, row_ids),
            (col_ids_hbm, col_ids), (coeffs_hbm, coeffs),
        ))
    ]
    for load in loads:
        load.start()
    r = lax.axis_index("row")
    c = lax.axis_index("col")
    n_z = n_row // 2
    z = r // 2
    x = lax.rem(r, 2)
    rows = nb * k
    grows = GROUP * k

    barrier = pltpu.get_barrier_semaphore()
    for d in range(1, n_row):
        pl.semaphore_signal(barrier, inc=1, device_id=(lax.rem(r + d, n_row), c), device_id_type=MESH)
    for d in range(1, n_col):
        pl.semaphore_signal(barrier, inc=1, device_id=(r, lax.rem(c + d, n_col)), device_id_type=MESH)

    def row_copy(phase, d, src, dst):
        return pltpu.make_async_remote_copy(
            src_ref=src, dst_ref=dst, send_sem=row_ssem.at[phase, d], recv_sem=row_rsem.at[phase, d],
            device_id=(lax.rem(r + d, n_row), c), device_id_type=MESH,
        )

    def col_copy(phase, d, src, dst):
        return pltpu.make_async_remote_copy(
            src_ref=src, dst_ref=dst, send_sem=col_ssem.at[phase, d], recv_sem=col_rsem.at[phase, d],
            device_id=(r, lax.rem(c + d, n_col)), device_id_type=MESH,
        )

    def x_copy(phase, sem, src, dst):
        return pltpu.make_async_remote_copy(
            src_ref=src, dst_ref=dst, send_sem=row_ssem.at[phase, sem], recv_sem=row_rsem.at[phase, sem],
            device_id=(z * 2 + 1 - x, c), device_id_type=MESH,
        )

    def z_copy(phase, d, sem, src, dst):
        return pltpu.make_async_remote_copy(
            src_ref=src, dst_ref=dst, send_sem=row_ssem.at[phase, sem], recv_sem=row_rsem.at[phase, sem],
            device_id=(lax.rem(z + d, n_z) * 2 + x, c), device_id_type=MESH,
        )

    def start_gather(phase, values):
        sent[phase] = values
        by_col = [
            col_copy(phase, d, sent.at[phase], row_g.at[phase, pl.ds(c * nb, nb)]) for d in range(1, n_col)
        ]
        own = col_g.at[phase, pl.ds(r * nb, nb)]
        by_z = [z_copy(phase, d, d, sent.at[phase], own) for d in range(1, n_z)]
        by_x = [x_copy(phase, n_z, sent.at[phase], own)]
        for copy in by_z + by_x + by_col:
            copy.start()
        row_g[phase, pl.ds(c * nb, nb)] = values
        col_g[phase, pl.ds(r * nb, nb)] = values
        return by_col, by_z, by_x

    def forward(phase, by_z):
        by_x = []
        for d in range(1, n_z):
            by_z[d - 1].wait_recv()
            piece = col_g.at[phase, pl.ds((lax.rem(z - d + n_z, n_z) * 2 + x) * nb, nb)]
            by_x.append(x_copy(phase, n_z + d, piece, piece))
            by_x[-1].start()
        for copy in by_z:
            copy.wait_send()
        return by_x

    def wait_all(copies):
        for copy in copies:
            copy.wait()

    live = live_smem[0, 0]

    def hot(ids, count):
        alive = lax.broadcasted_iota(jnp.int32, (count, slots), 1) < live
        same = lax.broadcasted_iota(jnp.int32, (count, slots), 0) == ids
        one = jnp.where(same & alive, 1.0, 0.0).astype(BF16)
        return jnp.concatenate([one, one], axis=1)

    def slot_products(phase, source, index, dot):
        def body(group, carry):
            for u in range(8):
                s = group * 8 + u
                terms[pl.ds(pl.multiple_of(s * k, k), k), :] = dot(source[phase, index[0, s]], blocks[s])
            return carry

        lax.fori_loop(0, slots // 8, body, 0)

    def slot_sums(hots, acc, count):
        for q in range(k):
            part = terms[pl.ds(q, slots, stride=k), :]
            high = part.astype(BF16)
            low = (part - high.astype(F32)).astype(BF16)
            acc[pl.ds(q, count, stride=k), :] = dot_n(hots, jnp.concatenate([high, low], axis=0))

    def send_parts(phase, acc, out, part, count, me, make):
        out[phase] = acc[...].astype(BF16).reshape(count * nb, k, BS)
        copies = [
            make(3 + phase, d, out.at[phase, pl.ds(lax.rem(me + d, count) * nb, nb)], part.at[phase, me])
            for d in range(1, count)
        ]
        for copy in copies:
            copy.start()
        part[phase, me] = out[phase, pl.ds(me * nb, nb)]
        return copies

    order = list(range(1, n_z)) + [0]

    def send_x(phase):
        col_send[phase] = col_acc[...].astype(BF16).reshape(n_row * nb, k, BS)
        copies = {}
        for d in order:
            there = (lax.rem(z + d, n_z) * 2 + 1 - x) * nb
            copies[d] = x_copy(3 + phase, d, col_send.at[phase, pl.ds(there, nb)], x_part.at[phase, d])
            copies[d].start()
        return copies

    def send_z(phase, by_x):
        copies = []
        for d in order:
            by_x[d].wait()
            here = (lax.rem(z + d, n_z) * 2 + x) * rows
            mine = col_acc[pl.ds(pl.multiple_of(here, rows), rows), :].reshape(nb, k, BS)
            both = (mine + x_part[phase, d].astype(F32)).astype(BF16)
            if d == 0:
                col_part[phase, 0] = both
            else:
                z_send[phase, d] = both
                copies.append(z_copy(3 + phase, d, n_z + d, z_send.at[phase, d], col_part.at[phase, d]))
                copies[-1].start()
        return copies

    def part_sum(phase, part, count):
        total = part[phase, 0].astype(F32)
        for i in range(1, count):
            total = total + part[phase, i].astype(F32)
        return total

    def inner(gathered, acc, count):
        total = jnp.zeros((k, BS), F32)
        for i in range(0, count * nb, GROUP):
            total = total + jnp.sum(
                gathered(i).astype(F32) * acc[i * k : (i + GROUP) * k, :].reshape(GROUP, k, BS), axis=0
            )
        return total

    def local_dot(left, right):
        return jnp.sum(left * right, axis=0)

    lane = lax.broadcasted_iota(jnp.int32, (k, BS), 1)

    def reduce_row(phase, num, den):
        packed = jnp.where(
            lane < BS // 2, jnp.sum(num, axis=1, keepdims=True), jnp.sum(den, axis=1, keepdims=True)
        )
        scal[0, phase] = packed
        row_scal[phase, r] = packed
        copies = [row_copy(5 + phase, d, scal.at[0, phase], row_scal.at[phase, r]) for d in range(1, n_row)]
        for copy in copies:
            copy.start()
        return copies

    def reduce_col(phase, copies):
        wait_all(copies)
        packed = jnp.sum(row_scal[phase], axis=0)
        scal[1, phase] = packed
        col_scal[phase, c] = packed
        copies = [col_copy(5 + phase, d, scal.at[1, phase], col_scal.at[phase, c]) for d in range(1, n_col)]
        for copy in copies:
            copy.start()
        wait_all(copies)
        total = jnp.sum(col_scal[phase], axis=0)
        return total[:, 0:1] / total[:, BS // 2 : BS // 2 + 1]

    def tiles(flat):
        return jnp.stack([flat[:, j * BS : (j + 1) * BS] for j in range(nb)], axis=0)

    loads[0].wait()
    start = block_in[...]
    block = tiles(start)
    pl.semaphore_wait(barrier, n_row + n_col - 2)
    by_col, by_z, by_x = start_gather(0, block.astype(BF16))
    for load in loads[1:]:
        load.wait()

    search = tiles(search_in[...])
    precond = precond_in[...].reshape(nb, 1, BS)
    diag = diag_in[...].reshape(nb, 1, BS)
    hot_rows = hot(row_ids[...], n_col * nb)
    hot_cols = hot(col_ids[...], n_row * nb)

    spread = (
        lax.broadcasted_iota(jnp.int32, (grows, k), 0) % k == lax.broadcasted_iota(jnp.int32, (grows, k), 1)
    ).astype(F32)
    same_group = (
        lax.broadcasted_iota(jnp.int32, (grows, grows), 0) // k
        == lax.broadcasted_iota(jnp.int32, (grows, grows), 1) // k
    )

    def expand(coef):
        wide = dot_t(dot_t(spread, coef, HI), spread, HI)
        return jnp.where(same_group, wide, 0.0)

    mats = [[expand(coeffs[i, j]) for j in range(3)] for i in range(ITERS)]

    def combine(mat, values):
        flat = values.reshape(rows, BS)
        return jnp.concatenate(
            [dot_n(mat, flat[i : i + grows], HI) for i in range(0, rows, grows)], axis=0
        ).reshape(nb, k, BS)

    def combine_gathered(mat, values):
        high = mat.astype(BF16)
        low = (mat - high.astype(F32)).astype(BF16)
        flat = values.reshape(grows, BS)
        return (dot_n(high, flat) + dot_n(low, flat)).reshape(GROUP, k, BS)

    def operator(phase, by_col, by_z, by_x, send):
        by_x = by_x + forward(phase, by_z)
        wait_all(by_col)
        slot_products(phase, row_g, row_smem, dot_n)
        slot_sums(hot_cols, col_acc, n_row * nb)
        row_parts = send_x(phase) if send else {}
        wait_all(by_x)
        slot_products(phase, col_g, col_smem, dot_t)
        slot_sums(hot_rows, row_acc, n_col * nb)
        col_parts = send_parts(phase, row_acc, row_send, row_part, n_col, c, col_copy) if send else []
        return row_parts, col_parts

    row_parts, col_parts = operator(0, by_col, by_z, by_x, True)
    own = diag * sent[0].astype(F32)
    num = (
        local_dot(block, own)
        + inner(lambda i: row_g[0, i : i + GROUP], row_acc, n_col)
        + inner(lambda i: col_g[0, i : i + GROUP], col_acc, n_row)
    )
    copies = reduce_row(0, num, local_dot(block, block))
    parts = send_z(0, row_parts) + col_parts
    ritz = reduce_col(0, copies)
    wait_all(parts)
    image = own + part_sum(0, row_part, n_col) + part_sum(0, col_part, n_z)

    for i in range(ITERS):
        mat_x, mat_w, mat_p = mats[i]
        phase = i + 1
        residual = (image - ritz[None] * block) * precond
        search = combine(mat_w, residual) + combine(mat_p, search)
        by_col, by_z, by_x = start_gather(phase, search.astype(BF16))
        block = combine(mat_x, block) + search
        own = diag * sent[phase].astype(F32)
        image = combine(mat_x, image) + own
        num = local_dot(block, image)
        den = local_dot(block, block)
        for gathered, total, count in ((row_g, row_b, n_col), (col_g, col_b, n_row)):
            for g in range(0, count * nb, GROUP):
                old = gathered[0, g : g + GROUP] if i == 0 else total[g : g + GROUP]
                total[g : g + GROUP] = combine_gathered(mat_x, old).astype(BF16)
        if i == ITERS - 1:
            for j in range(nb):
                block_out[:, j * BS : (j + 1) * BS] = block[j]
        row_parts, col_parts = operator(phase, by_col, by_z, by_x, i < ITERS - 1)
        for gathered, total, count in ((row_g, row_b, n_col), (col_g, col_b, n_row)):
            for g in range(0, count * nb, GROUP):
                total[g : g + GROUP] = (
                    total[g : g + GROUP].astype(F32) + gathered[phase, g : g + GROUP].astype(F32)
                ).astype(BF16)
        num = (
            num
            + inner(lambda g: row_b[g : g + GROUP], row_acc, n_col)
            + inner(lambda g: col_b[g : g + GROUP], col_acc, n_row)
        )
        copies = reduce_row(phase, num, den)
        parts = send_z(phase, row_parts) + col_parts if i < ITERS - 1 else []
        ritz = reduce_col(phase, copies)
        if i < ITERS - 1:
            wait_all(parts)
            image = image + part_sum(phase, row_part, n_col) + part_sum(phase, col_part, n_z)

    ritz_out[...] = jnp.broadcast_to(ritz, (k, BS))


def on_device(
    n_row, n_col, start_block, start_search, precond, diag_energy, blocks, row_index, col_index,
    live_count, ritz_coeffs,
):
    k, length = start_block.shape
    nb = length // BS
    slots = blocks.shape[2]
    phases = ITERS + 1
    vmem = pl.BlockSpec(memory_space=pltpu.VMEM)
    hbm = pl.BlockSpec(memory_space=pltpu.HBM)
    smem = pl.BlockSpec(memory_space=pltpu.SMEM)
    row_ids = row_index[0]
    col_ids = col_index[0]
    block, ritz = pl.pallas_call(
        functools.partial(kernel, n_row, n_col, nb, k, slots),
        out_shape=(
            jax.ShapeDtypeStruct((k, length), F32),
            jax.ShapeDtypeStruct((k, BS), F32),
        ),
        in_specs=[hbm] * 8 + [smem] * 3,
        out_specs=(vmem, vmem),
        scratch_shapes=[
            pltpu.VMEM((phases, nb, k, BS), BF16),
            pltpu.VMEM((phases, n_col * nb, k, BS), BF16),
            pltpu.VMEM((phases, n_row * nb, k, BS), BF16),
            pltpu.VMEM((n_col * nb, k, BS), BF16),
            pltpu.VMEM((n_row * nb, k, BS), BF16),
            pltpu.VMEM((slots * k, BS), F32),
            pltpu.VMEM((n_col * nb * k, BS), F32),
            pltpu.VMEM((n_row * nb * k, BS), F32),
            pltpu.VMEM((phases - 1, n_col * nb, k, BS), BF16),
            pltpu.VMEM((phases - 1, n_row * nb, k, BS), BF16),
            pltpu.VMEM((phases - 1, n_col, nb, k, BS), BF16),
            pltpu.VMEM((phases - 1, n_row // 2, nb, k, BS), BF16),
            pltpu.VMEM((2, phases, k, BS), F32),
            pltpu.VMEM((phases, n_row, k, BS), F32),
            pltpu.VMEM((phases, n_col, k, BS), F32),
            pltpu.VMEM((phases - 1, n_row // 2, nb, k, BS), BF16),
            pltpu.VMEM((phases - 1, n_row // 2, nb, k, BS), BF16),
            pltpu.SemaphoreType.DMA((8, n_row)),
            pltpu.SemaphoreType.DMA((8, n_row)),
            pltpu.SemaphoreType.DMA((8, n_col)),
            pltpu.SemaphoreType.DMA((8, n_col)),
            pltpu.VMEM((k, length), F32),
            pltpu.VMEM((k, length), F32),
            pltpu.VMEM((nb, BS), F32),
            pltpu.VMEM((nb, BS), F32),
            pltpu.VMEM((slots, BS, BS), BF16),
            pltpu.VMEM((1, slots), jnp.int32),
            pltpu.VMEM((1, slots), jnp.int32),
            pltpu.VMEM(ritz_coeffs.shape, F32),
            pltpu.SemaphoreType.DMA((8,)),
        ],
        compiler_params=pltpu.CompilerParams(
            collective_id=0, has_side_effects=True, vmem_limit_bytes=48 * 1024 * 1024
        ),
    )(
        start_block, start_search, precond.reshape(nb, BS), diag_energy.reshape(nb, BS), blocks[0, 0],
        row_ids, col_ids, ritz_coeffs, row_ids, col_ids, live_count,
    )
    return block, ritz[:, 0]


def solution(mesh):
    placed = (
        P(None, ("row", "col")),
        P(None, ("row", "col")),
        P(("row", "col")),
        P(("row", "col")),
        P("row", "col", None, None, None),
        P("row", "col", None),
        P("row", "col", None),
        P("row", "col"),
        P(),
    )
    return jax.shard_map(
        functools.partial(on_device, mesh.shape["row"], mesh.shape["col"]),
        mesh=mesh,
        in_specs=placed,
        out_specs=(P(None, ("row", "col")), P()),
        check_vma=False,
    )
```

```python
import functools

import jax
import jax.numpy as jnp
from jax import lax
from jax.experimental import pallas as pl
from jax.experimental.pallas import tpu as pltpu
from jax.sharding import PartitionSpec as P

ITERS = 2
BS = 128
GROUP = 9
F32 = jnp.float32
BF16 = jnp.bfloat16
HI = lax.Precision.HIGHEST
MESH = pl.DeviceIdType.MESH


def dot_t(left, right, precision=None):
    return lax.dot_general(
        left, right, (((1,), (1,)), ((), ())), precision=precision, preferred_element_type=F32
    )


def dot_n(left, right, precision=None):
    return lax.dot_general(
        left, right, (((1,), (0,)), ((), ())), precision=precision, preferred_element_type=F32
    )


def kernel(
    n_row, n_col, nb, k, slots,
    block_hbm, search_hbm, precond_hbm, diag_hbm, blocks_hbm, row_ids_hbm, col_ids_hbm, coeffs_hbm,
    row_smem, col_smem, live_smem,
    block_out, ritz_out,
    sent, row_g0, row_g1, row_g2, col_g0, col_g1, col_g2, row_b, col_b, terms, row_acc, col_acc, row_send, col_send,
    row_part, col_part, scal, row_scal, col_scal,
    x_part, z_send, row_ssem, row_rsem, col_ssem, col_rsem,
    block_in, search_in, precond_in, diag_in, blocks, row_ids, col_ids, coeffs, load_sem,
):
    loads = [
        pltpu.make_async_copy(src, dst, load_sem.at[i])
        for i, (src, dst) in enumerate((
            (block_hbm, block_in), (search_hbm, search_in), (precond_hbm, precond_in),
            (diag_hbm, diag_in), (blocks_hbm, blocks), (row_ids_hbm, row_ids),
            (col_ids_hbm, col_ids), (coeffs_hbm, coeffs),
        ))
    ]
    for load in loads:
        load.start()
    r = lax.axis_index("row")
    c = lax.axis_index("col")
    row_g = (row_g0, row_g1, row_g2)
    col_g = (col_g0, col_g1, col_g2)
    n_z = n_row // 2
    z = r // 2
    x = lax.rem(r, 2)
    rows = nb * k
    grows = GROUP * k

    barrier = pltpu.get_barrier_semaphore()
    for d in range(1, n_row):
        pl.semaphore_signal(barrier, inc=1, device_id=(lax.rem(r + d, n_row), c), device_id_type=MESH)
    for d in range(1, n_col):
        pl.semaphore_signal(barrier, inc=1, device_id=(r, lax.rem(c + d, n_col)), device_id_type=MESH)

    def row_copy(phase, d, src, dst):
        return pltpu.make_async_remote_copy(
            src_ref=src, dst_ref=dst, send_sem=row_ssem.at[phase, d], recv_sem=row_rsem.at[phase, d],
            device_id=(lax.rem(r + d, n_row), c), device_id_type=MESH,
        )

    def col_copy(phase, d, src, dst):
        return pltpu.make_async_remote_copy(
            src_ref=src, dst_ref=dst, send_sem=col_ssem.at[phase, d], recv_sem=col_rsem.at[phase, d],
            device_id=(r, lax.rem(c + d, n_col)), device_id_type=MESH,
        )

    def x_copy(phase, sem, src, dst):
        return pltpu.make_async_remote_copy(
            src_ref=src, dst_ref=dst, send_sem=row_ssem.at[phase, sem], recv_sem=row_rsem.at[phase, sem],
            device_id=(z * 2 + 1 - x, c), device_id_type=MESH,
        )

    def z_copy(phase, d, sem, src, dst):
        return pltpu.make_async_remote_copy(
            src_ref=src, dst_ref=dst, send_sem=row_ssem.at[phase, sem], recv_sem=row_rsem.at[phase, sem],
            device_id=(lax.rem(z + d, n_z) * 2 + x, c), device_id_type=MESH,
        )

    def start_gather(phase, values):
        sent[phase] = values
        by_col = [
            col_copy(phase, d, sent.at[phase], row_g[phase].at[pl.ds(c * nb, nb)]) for d in range(1, n_col)
        ]
        own = col_g[phase].at[pl.ds(r * nb, nb)]
        by_z = [z_copy(phase, d, d, sent.at[phase], own) for d in range(1, n_z)]
        by_x = [x_copy(phase, n_z, sent.at[phase], own)]
        for copy in by_z + by_x + by_col:
            copy.start()
        row_g[phase][pl.ds(c * nb, nb)] = values
        col_g[phase][pl.ds(r * nb, nb)] = values
        return by_col, by_z, by_x

    def forward(phase, by_z):
        by_x = []
        for d in range(1, n_z):
            by_z[d - 1].wait_recv()
            piece = col_g[phase].at[pl.ds((lax.rem(z - d + n_z, n_z) * 2 + x) * nb, nb)]
            by_x.append(x_copy(phase, n_z + d, piece, piece))
            by_x[-1].start()
        for copy in by_z:
            copy.wait_send()
        return by_x

    def wait_all(copies):
        for copy in copies:
            copy.wait()

    live = live_smem[0, 0]

    def hot(ids, count):
        alive = lax.broadcasted_iota(jnp.int32, (count, slots), 1) < live
        same = lax.broadcasted_iota(jnp.int32, (count, slots), 0) == ids
        one = jnp.where(same & alive, 1.0, 0.0).astype(BF16)
        return jnp.concatenate([one, one], axis=1)

    def slot_products(phase, source, index, dot):
        def body(group, carry):
            for u in range(8):
                s = group * 8 + u
                terms[pl.ds(pl.multiple_of(s * k, k), k), :] = dot(source[phase][index[0, s]], blocks[s])
            return carry

        lax.fori_loop(0, slots // 8, body, 0)

    def slot_sums(hots, acc, count):
        for q in range(k):
            part = terms[pl.ds(q, slots, stride=k), :]
            high = part.astype(BF16)
            low = (part - high.astype(F32)).astype(BF16)
            acc[pl.ds(q, count, stride=k), :] = dot_n(hots, jnp.concatenate([high, low], axis=0))

    def send_parts(phase, acc, out, part, count, me, make):
        out[phase] = acc[...].astype(BF16).reshape(count * nb, k, BS)
        copies = [
            make(3 + phase, d, out.at[phase, pl.ds(lax.rem(me + d, count) * nb, nb)], part.at[phase, me])
            for d in range(1, count)
        ]
        for copy in copies:
            copy.start()
        part[phase, me] = out[phase, pl.ds(me * nb, nb)]
        return copies

    order = list(range(1, n_z)) + [0]

    def send_x(phase):
        col_send[phase] = col_acc[...].astype(BF16).reshape(n_row * nb, k, BS)
        copies = {}
        for d in order:
            there = (lax.rem(z + d, n_z) * 2 + 1 - x) * nb
            copies[d] = x_copy(3 + phase, d, col_send.at[phase, pl.ds(there, nb)], x_part.at[phase, d])
            copies[d].start()
        return copies

    def send_z(phase, by_x):
        copies = []
        for d in order:
            by_x[d].wait()
            here = (lax.rem(z + d, n_z) * 2 + x) * rows
            mine = col_acc[pl.ds(pl.multiple_of(here, rows), rows), :].reshape(nb, k, BS)
            both = (mine + x_part[phase, d].astype(F32)).astype(BF16)
            if d == 0:
                col_part[phase, 0] = both
            else:
                z_send[phase, d] = both
                copies.append(z_copy(3 + phase, d, n_z + d, z_send.at[phase, d], col_part.at[phase, d]))
                copies[-1].start()
        return copies

    def part_sum(phase, part, count):
        total = part[phase, 0].astype(F32)
        for i in range(1, count):
            total = total + part[phase, i].astype(F32)
        return total

    def inner(gathered, acc, count):
        total = jnp.zeros((k, BS), F32)
        for i in range(0, count * nb, GROUP):
            total = total + jnp.sum(
                gathered(i).astype(F32) * acc[i * k : (i + GROUP) * k, :].reshape(GROUP, k, BS), axis=0
            )
        return total

    def local_dot(left, right):
        return jnp.sum(left * right, axis=0)

    lane = lax.broadcasted_iota(jnp.int32, (k, BS), 1)

    def reduce_row(phase, num, den):
        packed = jnp.where(
            lane < BS // 2, jnp.sum(num, axis=1, keepdims=True), jnp.sum(den, axis=1, keepdims=True)
        )
        scal[0, phase] = packed
        row_scal[phase, r] = packed
        copies = [row_copy(5 + phase, d, scal.at[0, phase], row_scal.at[phase, r]) for d in range(1, n_row)]
        for copy in copies:
            copy.start()
        return copies

    def reduce_col(phase, copies):
        wait_all(copies)
        packed = jnp.sum(row_scal[phase], axis=0)
        scal[1, phase] = packed
        col_scal[phase, c] = packed
        copies = [col_copy(5 + phase, d, scal.at[1, phase], col_scal.at[phase, c]) for d in range(1, n_col)]
        for copy in copies:
            copy.start()
        wait_all(copies)
        total = jnp.sum(col_scal[phase], axis=0)
        return total[:, 0:1] / total[:, BS // 2 : BS // 2 + 1]

    def tiles(flat):
        return jnp.stack([flat[:, j * BS : (j + 1) * BS] for j in range(nb)], axis=0)

    loads[0].wait()
    start = block_in[...]
    block = tiles(start)
    pl.semaphore_wait(barrier, n_row + n_col - 2)
    by_col, by_z, by_x = start_gather(0, block.astype(BF16))
    for load in loads[1:]:
        load.wait()

    search = tiles(search_in[...])
    precond = precond_in[...].reshape(nb, 1, BS)
    diag = diag_in[...].reshape(nb, 1, BS)
    hot_rows = hot(row_ids[...], n_col * nb)
    hot_cols = hot(col_ids[...], n_row * nb)

    spread = (
        lax.broadcasted_iota(jnp.int32, (grows, k), 0) % k == lax.broadcasted_iota(jnp.int32, (grows, k), 1)
    ).astype(F32)
    same_group = (
        lax.broadcasted_iota(jnp.int32, (grows, grows), 0) // k
        == lax.broadcasted_iota(jnp.int32, (grows, grows), 1) // k
    )

    def expand(coef):
        wide = dot_t(dot_t(spread, coef, HI), spread, HI)
        return jnp.where(same_group, wide, 0.0)

    mats = [[expand(coeffs[i, j]) for j in range(3)] for i in range(ITERS)]

    def combine(mat, values):
        flat = values.reshape(rows, BS)
        return jnp.concatenate(
            [dot_n(mat, flat[i : i + grows], HI) for i in range(0, rows, grows)], axis=0
        ).reshape(nb, k, BS)

    def combine_gathered(mat, values):
        high = mat.astype(BF16)
        low = (mat - high.astype(F32)).astype(BF16)
        flat = values.reshape(grows, BS)
        return (dot_n(high, flat) + dot_n(low, flat)).reshape(GROUP, k, BS)

    def operator(phase, by_col, by_z, by_x, send, early=None):
        by_x = by_x + forward(phase, by_z)
        wait_all(by_col)
        slot_products(phase, row_g, row_smem, dot_n)
        slot_sums(hot_cols, col_acc, n_row * nb)
        row_parts = send_x(phase) if send else {}
        wait_all(by_x)
        early_copies = early() if early else []
        slot_products(phase, col_g, col_smem, dot_t)
        slot_sums(hot_rows, row_acc, n_col * nb)
        col_parts = send_parts(phase, row_acc, row_send, row_part, n_col, c, col_copy) if send else []
        return row_parts, col_parts, early_copies

    own = diag * sent[0].astype(F32)

    def early():
        num = local_dot(block, own) + 2.0 * inner(lambda i: col_g[0][i : i + GROUP], col_acc, n_row)
        return reduce_row(0, num, local_dot(block, block))

    row_parts, col_parts, copies = operator(0, by_col, by_z, by_x, True, early)
    parts = send_z(0, row_parts) + col_parts
    ritz = reduce_col(0, copies)
    wait_all(parts)
    image = own + part_sum(0, row_part, n_col) + part_sum(0, col_part, n_z)

    for i in range(ITERS):
        mat_x, mat_w, mat_p = mats[i]
        phase = i + 1
        residual = (image - ritz[None] * block) * precond
        search = combine(mat_w, residual) + combine(mat_p, search)
        by_col, by_z, by_x = start_gather(phase, search.astype(BF16))
        block = combine(mat_x, block) + search
        own = diag * sent[phase].astype(F32)
        image = combine(mat_x, image) + own
        num = local_dot(block, image)
        den = local_dot(block, block)
        for gathered, total, count in ((row_g, row_b, n_col), (col_g, col_b, n_row)):
            for g in range(0, count * nb, GROUP):
                old = gathered[0][g : g + GROUP] if i == 0 else total[g : g + GROUP]
                total[g : g + GROUP] = combine_gathered(mat_x, old).astype(BF16)
        if i == ITERS - 1:
            for j in range(nb):
                block_out[:, j * BS : (j + 1) * BS] = block[j]
        row_parts, col_parts, _ = operator(phase, by_col, by_z, by_x, i < ITERS - 1)
        for gathered, total, count in ((row_g, row_b, n_col), (col_g, col_b, n_row)):
            for g in range(0, count * nb, GROUP):
                total[g : g + GROUP] = (
                    total[g : g + GROUP].astype(F32) + gathered[phase][g : g + GROUP].astype(F32)
                ).astype(BF16)
        num = (
            num
            + inner(lambda g: row_b[g : g + GROUP], row_acc, n_col)
            + inner(lambda g: col_b[g : g + GROUP], col_acc, n_row)
        )
        copies = reduce_row(phase, num, den)
        parts = send_z(phase, row_parts) + col_parts if i < ITERS - 1 else []
        ritz = reduce_col(phase, copies)
        if i < ITERS - 1:
            wait_all(parts)
            image = image + part_sum(phase, row_part, n_col) + part_sum(phase, col_part, n_z)

    ritz_out[...] = jnp.broadcast_to(ritz, (k, BS))


def on_device(
    n_row, n_col, start_block, start_search, precond, diag_energy, blocks, row_index, col_index,
    live_count, ritz_coeffs,
):
    k, length = start_block.shape
    nb = length // BS
    slots = blocks.shape[2]
    phases = ITERS + 1
    vmem = pl.BlockSpec(memory_space=pltpu.VMEM)
    hbm = pl.BlockSpec(memory_space=pltpu.HBM)
    smem = pl.BlockSpec(memory_space=pltpu.SMEM)
    row_ids = row_index[0]
    col_ids = col_index[0]
    block, ritz = pl.pallas_call(
        functools.partial(kernel, n_row, n_col, nb, k, slots),
        out_shape=(
            jax.ShapeDtypeStruct((k, length), F32),
            jax.ShapeDtypeStruct((k, BS), F32),
        ),
        in_specs=[hbm] * 8 + [smem] * 3,
        out_specs=(vmem, vmem),
        scratch_shapes=[
            pltpu.VMEM((phases, nb, k, BS), BF16),
            *[pltpu.VMEM((n_col * nb, k, BS), BF16)] * phases,
            *[pltpu.VMEM((n_row * nb, k, BS), BF16)] * phases,
            pltpu.VMEM((n_col * nb, k, BS), BF16),
            pltpu.VMEM((n_row * nb, k, BS), BF16),
            pltpu.VMEM((slots * k, BS), F32),
            pltpu.VMEM((n_col * nb * k, BS), F32),
            pltpu.VMEM((n_row * nb * k, BS), F32),
            pltpu.VMEM((phases - 1, n_col * nb, k, BS), BF16),
            pltpu.VMEM((phases - 1, n_row * nb, k, BS), BF16),
            pltpu.VMEM((phases - 1, n_col, nb, k, BS), BF16),
            pltpu.VMEM((phases - 1, n_row // 2, nb, k, BS), BF16),
            pltpu.VMEM((2, phases, k, BS), F32),
            pltpu.VMEM((phases, n_row, k, BS), F32),
            pltpu.VMEM((phases, n_col, k, BS), F32),
            pltpu.VMEM((phases - 1, n_row // 2, nb, k, BS), BF16),
            pltpu.VMEM((phases - 1, n_row // 2, nb, k, BS), BF16),
            pltpu.SemaphoreType.DMA((8, n_row)),
            pltpu.SemaphoreType.DMA((8, n_row)),
            pltpu.SemaphoreType.DMA((8, n_col)),
            pltpu.SemaphoreType.DMA((8, n_col)),
            pltpu.VMEM((k, length), F32),
            pltpu.VMEM((k, length), F32),
            pltpu.VMEM((nb, BS), F32),
            pltpu.VMEM((nb, BS), F32),
            pltpu.VMEM((slots, BS, BS), BF16),
            pltpu.VMEM((1, slots), jnp.int32),
            pltpu.VMEM((1, slots), jnp.int32),
            pltpu.VMEM(ritz_coeffs.shape, F32),
            pltpu.SemaphoreType.DMA((8,)),
        ],
        compiler_params=pltpu.CompilerParams(
            collective_id=0, has_side_effects=True, vmem_limit_bytes=48 * 1024 * 1024
        ),
    )(
        start_block, start_search, precond.reshape(nb, BS), diag_energy.reshape(nb, BS), blocks[0, 0],
        row_ids, col_ids, ritz_coeffs, row_ids, col_ids, live_count,
    )
    return block, ritz[:, 0]


def solution(mesh):
    placed = (
        P(None, ("row", "col")),
        P(None, ("row", "col")),
        P(("row", "col")),
        P(("row", "col")),
        P("row", "col", None, None, None),
        P("row", "col", None),
        P("row", "col", None),
        P("row", "col"),
        P(),
    )
    return jax.shard_map(
        functools.partial(on_device, mesh.shape["row"], mesh.shape["col"]),
        mesh=mesh,
        in_specs=placed,
        out_specs=(P(None, ("row", "col")), P()),
        check_vma=False,
    )
```
